256 devices in a mesh: pair: 16 (over z, core), ri: 16 (over y, x).
Axes of the slice: x: 4, y: 4, z: 8, core: 2. Of those that a mesh axis runs over, the one named last changes fastest.
Arguments:
- three_center: bfloat16 [16, 2048, 16, 384], P('pair', 'ri'), may hold values from -6 to 6
- green: bfloat16 [16, 16, 64, 64], P('pair'), may hold values from -0.3125 to 0.3125
- screened: bfloat16 [2048, 2048], P('ri'), may hold values from -0.00015258789 to 0.00015258789
- block_tile: int32 [16, 6], replicated, may hold values from 0 to 15, all different within a row
- sigma_owner: int32 [16], replicated, may hold values from 0 to 15, as said below
Outputs:
- sigma: float32 [16, 16, 16], P('pair')
The draws below stay inside these ranges and needn't reach their ends.
Inputs may be any that keep to these rules, and one draw needn't show every extreme that they name: `block_tile`: each row names 6 different tiles; every one of the 16 tiles is named by some region. `sigma_owner`: each owner slot appears once.
All inputs are finite; a program needn't handle non-finite values.
Results may differ from the reference program's by a relative error of at most 0.0041.
Values may be sent and summed in bfloat16 or wider, within the bound.
A program may use at most 128 MiB of HBM per device.

```python
import jax
import jax.numpy as jnp
from jax import lax

NRI = 2048
MU = 16
AT = 64
KB = 6
NTL = 16
N_PAIR = 16


def place_slot(order, position, target):
    indices = jnp.arange(order.shape[0], dtype=jnp.int32)
    holder = jnp.sum(jnp.where(order == target, indices, 0)).astype(jnp.int32)
    current = order[position]
    order = order.at[holder].set(current)
    return order.at[position].set(target)


def draw_sigma_owner(key, part):
    key = jax.random.fold_in(key, 7)
    key_order, key_start = jax.random.split(key)
    order = jax.random.permutation(key_order, jnp.arange(N_PAIR, dtype=jnp.int32))
    start = jax.random.randint(key_start, (), 0, N_PAIR, dtype=jnp.int32)
    order = place_slot(order, start, (start + N_PAIR // 2) % N_PAIR)
    second = (start + 1) % N_PAIR
    order = place_slot(order, second, (second + 1) % N_PAIR)
    return order.astype(jnp.int32)


def block_scale(own_key, extent, cuts, low, high):
    factor_of = 1.0
    for dim, shards_of in cuts:
        steps = jax.random.uniform(jax.random.fold_in(jax.random.fold_in(own_key, 6), dim), (shards_of,), jnp.float32, low / len(cuts), high / len(cuts))
        factor_of = factor_of * jnp.repeat(jnp.exp(steps), extent[dim] // shards_of).reshape((-1,) + (1,) * (len(extent) - 1 - dim))
    return factor_of


def choose_distinct(stream_key, rows, number_of, top, lift):
    ranking = jax.random.permutation(jax.random.fold_in(stream_key, 1), number_of)
    favour = ranking
    for power in range(3):
        favour = favour * favour // number_of
    favour = favour * lift // number_of
    chance = jax.random.randint(jax.random.fold_in(stream_key, 2), (rows, number_of), 0, 4096) + favour
    fixed_rows = jax.random.permutation(jax.random.fold_in(stream_key, 3), rows)[jnp.arange(number_of) % rows]
    chance = jnp.where(jnp.arange(rows)[:, None] == fixed_rows[None, :], 1 << 14, chance)
    priority = chance * number_of + jnp.arange(number_of)
    return lax.top_k(priority.astype(jnp.int32), top)[1].astype(jnp.int32)


def noise(own_key, extent, scale, limit, pieces=(), held_as=jnp.bfloat16):
    factor_of = block_scale(own_key, extent, pieces, -0.22, 0.18) if pieces else 1.0
    drawn = jax.random.normal(own_key, extent, jnp.float32) * scale * factor_of
    return jnp.minimum(jnp.maximum(drawn, -limit), limit).astype(held_as)


def setup_inputs(seed: int = 0) -> dict:
    key_list = jax.random.split(jax.random.key(seed), 6)
    return {
        "three_center": noise(key_list[0], (N_PAIR, NRI, MU, KB * AT), 1.0, 6.0, ((0, 16), (1, 16))),
        "green": noise(key_list[1], (NTL, NTL, AT, AT), (KB * AT) ** -0.5, 0.3125, ((0, 16),)),
        "screened": noise(key_list[2], (NRI, NRI), (NRI * NRI * KB * AT) ** -0.5, 0.00015258789, ((0, 16),)),
        "block_tile": choose_distinct(key_list[3], N_PAIR, NTL, KB, 6144),
        "sigma_owner": draw_sigma_owner(jax.random.fold_in(key_list[5], 71), 0),
    }


def reference(three_center, green, screened, block_tile, sigma_owner):
    columns = KB * AT

    def one_region(inputs):
        tiles, tensor = inputs
        selected = jnp.take(jnp.take(green, tiles, axis=0), tiles, axis=1)
        coupling = selected.transpose(0, 2, 1, 3).reshape(columns, columns)
        flat = tensor.reshape(NRI * MU, columns)
        half = jnp.dot(flat, coupling, preferred_element_type=jnp.float32).astype(jnp.bfloat16)
        half = half.reshape(NRI, MU, columns)
        weighted = jnp.dot(screened, tensor.reshape(NRI, MU * columns), preferred_element_type=jnp.float32)
        weighted = weighted.astype(jnp.bfloat16).reshape(NRI, MU, columns)
        return -jnp.einsum("pmc,pnc->mn", half.astype(jnp.float32), weighted.astype(jnp.float32))

    tiles_all = lax.map(one_region, (block_tile, three_center))
    return jnp.zeros_like(tiles_all).at[sigma_owner].set(tiles_all)
```

```python
import functools

import jax
import jax.numpy as jnp
from jax import lax
from jax.experimental import pallas as pl
from jax.experimental.pallas import tpu as pltpu
from jax.sharding import PartitionSpec as P

MESH = pl.DeviceIdType.MESH
F32, BF16 = jnp.float32, jnp.bfloat16


def remote(src, dst, send_sem, recv_sem, device):
    return pltpu.make_async_remote_copy(
        src_ref=src, dst_ref=dst, send_sem=send_sem, recv_sem=recv_sem, device_id=device, device_id_type=MESH
    )


def wait_bytes(ref, sem):
    pltpu.make_async_copy(ref, ref, sem).wait()


def iota2(shape, dim):
    return lax.broadcasted_iota(jnp.int32, shape, dim)


def kernel(
    tiles_ref, owner_ref, three_hbm, green_hbm, screened_hbm, out_ref,
    three, green, by_mu, columns, rows, weighted, arrived, half, greens, coupling, gram, partials, totals,
    local_sem, a_send, a_recv, t_send, t_recv, ring_send, ring_recv, sib_send, sib_recv, own_send, own_recv,
    g_ring_send, g_ring_recv, g_sib_send, g_sib_recv, g_own_send, g_own_recv,
    w_send, w_recv, f_send, f_recv,
):
    pair, ri = lax.axis_index("pair"), lax.axis_index("ri")
    z, core = pair // 2, pair % 2
    sibling = (z * 2 + 1 - core, ri)

    def chip(step):
        return (z + step + 8) % 8

    def neighbour(step):
        return (chip(step) * 2 + core, ri)

    def plane_peer(step):
        return (ri + step) % 16

    load_three = pltpu.make_async_copy(three_hbm.at[0], three, local_sem.at[0])
    load_green = pltpu.make_async_copy(green_hbm.at[0], green, local_sem.at[1])
    mine = pl.ds(pl.multiple_of(ri * 16, 16), 16)
    row_piece = screened_hbm.at[
        pl.ds(pl.multiple_of(z * 16, 16), 16), pl.ds(pl.multiple_of(core * 1024, 1024), 1024)
    ]
    load_rows = pltpu.make_async_copy(row_piece, rows.at[z, core, mine], local_sem.at[2])
    load_three.start()
    load_green.start()
    load_rows.start()
    barrier = pltpu.get_barrier_semaphore()

    @pl.loop(1, 16)
    def _(step):
        pl.semaphore_signal(barrier, inc=1, device_id=(pair, plane_peer(step)), device_id_type=MESH)
        pl.semaphore_signal(barrier, inc=1, device_id=((pair + step) % 16, ri), device_id_type=MESH)

    first, second = iota2((256, 256), 0), iota2((256, 256), 1)
    swap = ((first % 16) * 16 + first // 16 == second).astype(BF16)
    load_three.wait()

    @pl.loop(0, 8)
    def _(chunk):
        at = pl.ds(pl.multiple_of(chunk * 16, 16), 16)
        block = three[at].reshape(256, 384)
        by_mu[:, at] = jnp.dot(swap, block, preferred_element_type=F32).astype(BF16).reshape(16, 16, 384)

    load_green.wait()
    for t in range(0, 16, 2):
        greens[pair, :, t * 64:(t + 2) * 64] = jnp.concatenate([green[t], green[t + 1]], axis=1)
    load_rows.wait()
    pl.semaphore_wait(barrier, 30)

    @pl.loop(1, 16)
    def _(step):
        remote(row_piece, rows.at[z, core, mine], a_send, a_recv, (pair, plane_peer(step))).start()

    def g_row(step, which):
        return greens.at[chip(step) * 2 + which]

    def g_send(way, step):
        i = (1 - way) // 2
        part = g_row(-way * (step - 1), core)
        if step == 4:
            part = part.at[pl.ds(i * 32, 32)]
        return remote(part, part, g_ring_send.at[i, step - 1], g_ring_recv.at[i, step - 1], neighbour(way))

    def g_arrival(way, step):
        i = (1 - way) // 2
        part = g_row(-way * step, core)
        if step == 4:
            part = part.at[pl.ds(i * 32, 32)]
        return part, g_ring_recv.at[i, step - 1]

    def g_side(way, step, which):
        i = (1 - way) // 2
        part = g_row(-way * step, which)
        if step == 4:
            part = part.at[pl.ds(i * 32, 32)]
        return remote(part, part, g_sib_send.at[i, step - 1], g_sib_recv.at[i, step - 1], sibling)

    g_own = remote(greens.at[pair], greens.at[pair], g_own_send, g_own_recv, sibling)
    g_send(1, 1).start()
    g_send(-1, 1).start()
    g_own.start()

    own_columns = pl.ds(pl.multiple_of(ri * 128, 128), 128)

    @pl.loop(1, 16)
    def _(step):
        peer = plane_peer(step)
        remote(by_mu.at[peer], columns.at[own_columns], t_send, t_recv, (pair, peer)).start()

    columns[own_columns, :] = by_mu[ri]

    def part_of(step, which, part):
        return rows.at[chip(step), which, pl.ds(part * 128, 128)]

    def ring(way, step, part):
        i = (1 - way) // 2
        ref = part_of(-way * (step - 1), core, part)
        return remote(ref, ref, ring_send.at[i, step - 1, part], ring_recv.at[i, step - 1, part], neighbour(way))

    def side(way, step, part, which):
        i = (1 - way) // 2
        ref = part_of(-way * step, which, part)
        return remote(ref, ref, sib_send.at[i, step - 1, part], sib_recv.at[i, step - 1, part], sibling)

    def parts_at(way, step):
        return (0, 1) if step < 4 else ((0,) if way == 1 else (1,))

    wait_bytes(rows.at[z, core, pl.ds(0, 240)], a_recv)
    own = remote(rows.at[z, core], rows.at[z, core], own_send, own_recv, sibling)
    for part in (0, 1):
        for way in (1, -1):
            ring(way, 1, part).start()
    own.start()

    def serve(step):
        for way in (1, -1):
            ref, sem = g_arrival(way, step)
            wait_bytes(ref, sem)
            if step < 4:
                g_send(way, step + 1).start()
            g_side(way, step, core).start()
        for part in (0, 1):
            for way in (1, -1):
                if part in parts_at(way, step):
                    i = (1 - way) // 2
                    wait_bytes(part_of(-way * step, core, part), ring_recv.at[i, step - 1, part])
                    if step < 4 and part in parts_at(way, step + 1):
                        ring(way, step + 1, part).start()
                    side(way, step, part, core).start()

    def sides_in(way, step):
        for part in parts_at(way, step):
            wait_bytes(part_of(-way * step, 1 - core, part), sib_recv.at[(1 - way) // 2, step - 1, part])

    def process(step):
        piece = chip(step)
        total = jnp.dot(rows[piece, 0], columns[0:1024], preferred_element_type=F32)
        total += jnp.dot(rows[piece, 1], columns[1024:2048], preferred_element_type=F32)
        weighted[piece] = total.astype(BF16)
        arrived[piece, mine] = weighted[piece, mine]

        @pl.loop(1, 16)
        def _(offset):
            peer = plane_peer(offset)
            at = pl.ds(pl.multiple_of(peer * 16, 16), 16)
            remote(
                weighted.at[piece, at], arrived.at[piece, mine], w_send.at[piece], w_recv.at[piece], (pair, peer)
            ).start()

    def collect(step):
        piece = chip(step)
        wait_bytes(arrived.at[piece, pl.ds(0, 240)], w_recv.at[piece])
        gram[...] += lax.dot_general(
            half[piece], arrived[piece], (((1,), (1,)), ((), ())), preferred_element_type=F32
        )

    serve(1)
    wait_bytes(columns.at[pl.ds(0, 1920)], t_recv)
    wait_bytes(rows.at[z, 1 - core], own_recv)
    process(0)
    for way in (1, -1):
        sides_in(way, 1)
        process(-way)
    serve(2)
    for way in (1, -1):
        sides_in(way, 2)
        process(-2 * way)
    serve(3)
    for way in (1, -1):
        sides_in(way, 3)
        process(-3 * way)

    wait_bytes(greens.at[z * 2 + 1 - core], g_own_recv)
    for step in (1, 2, 3):
        for way in (1, -1):
            wait_bytes(g_row(-way * step, 1 - core), g_sib_recv.at[(1 - way) // 2, step - 1])
    serve(4)
    for way in (1, -1):
        i = (1 - way) // 2
        wait_bytes(g_row(4, 1 - core).at[pl.ds(i * 32, 32)], g_sib_recv.at[i, 3])
    tile_of, lane_of = iota2((1024, 384), 0), iota2((1024, 384), 1)
    wanted = jnp.zeros((1024, 384), jnp.int32)
    for k in range(6):
        wanted = jnp.where(lane_of // 64 == k, tiles_ref[pair, k], wanted)
    select = ((tile_of // 64 == wanted) & (tile_of % 64 == lane_of % 64)).astype(BF16)
    for k in range(6):
        row = greens[tiles_ref[pair, k]]
        coupling[k * 64:(k + 1) * 64, :] = jnp.dot(row, select, preferred_element_type=F32).astype(BF16)

    @pl.loop(0, 8)
    def _(chunk):
        at = pl.ds(pl.multiple_of(chunk * 16, 16), 16)
        block = by_mu[:, at].reshape(256, 384)
        half[chunk] = jnp.dot(block, coupling[...], preferred_element_type=F32).astype(BF16)

    gram[...] = jnp.zeros_like(gram)
    for way in (1, -1):
        sides_in(way, 4)
    process(4)
    for step in (0, -1, 1, -2, 2, -3, 3, 4):
        collect(step)

    masked = jnp.where(first % 16 == second % 16, gram[...], 0.0)
    folded = jnp.sum(masked.reshape(16, 16, 256), axis=1)
    to_tile = (iota2((256, 128), 0) // 16 == iota2((256, 128), 1)).astype(F32)
    partials[ri] = jnp.dot(folded, to_tile, preferred_element_type=F32, precision=lax.Precision.HIGHEST)

    @pl.loop(1, 16)
    def _(step):
        remote(partials.at[ri], partials.at[ri], f_send.at[0], f_recv.at[0], (pair, plane_peer(step))).start()

    wait_bytes(partials.at[pl.ds(0, 15)], f_recv.at[0])
    totals[pair] = -jnp.sum(partials[...], axis=0)

    @pl.loop(1, 16)
    def _(step):
        remote(totals.at[pair], totals.at[pair], f_send.at[1], f_recv.at[1], ((pair + step) % 16, ri)).start()

    wait_bytes(rows.at[z, core, pl.ds(0, 240)], a_send)
    wait_bytes(columns.at[pl.ds(0, 1920)], t_send)
    own.wait_send()
    g_own.wait_send()
    for step in (1, 2, 3, 4):
        for way in (1, -1):
            g_send(way, step).wait_send()
            g_side(way, step, core).wait_send()
            for part in parts_at(way, step):
                ring(way, step, part).wait_send()
                side(way, step, part, core).wait_send()

    @pl.loop(0, 8)
    def _(piece):
        wait_bytes(weighted.at[piece, pl.ds(0, 240)], w_send.at[piece])

    wait_bytes(partials.at[pl.ds(0, 15)], f_send.at[0])
    wait_bytes(totals.at[pl.ds(0, 15)], f_send.at[1])
    wait_bytes(totals.at[pl.ds(0, 15)], f_recv.at[1])
    result = jnp.zeros((16, 128), F32)
    for region in range(16):
        result += jnp.where(owner_ref[region] == pair, totals[region], 0.0)
    out_ref[0] = result[:, 0:16]


def on_device(three_center, green, screened, block_tile, sigma_owner):
    dma = pltpu.SemaphoreType.DMA
    return pl.pallas_call(
        kernel,
        out_shape=jax.ShapeDtypeStruct((1, 16, 16), F32),
        in_specs=[pl.BlockSpec(memory_space=pltpu.SMEM)] * 2 + [pl.BlockSpec(memory_space=pl.ANY)] * 3,
        out_specs=pl.BlockSpec(memory_space=pltpu.VMEM),
        scratch_shapes=[
            pltpu.VMEM((128, 16, 384), BF16),
            pltpu.VMEM((16, 64, 64), BF16),
            pltpu.VMEM((16, 128, 384), BF16),
            pltpu.VMEM((2048, 384), BF16),
            pltpu.VMEM((8, 2, 256, 1024), BF16),
            pltpu.VMEM((8, 256, 384), BF16),
            pltpu.VMEM((8, 256, 384), BF16),
            pltpu.VMEM((8, 256, 384), BF16),
            pltpu.VMEM((16, 64, 1024), BF16),
            pltpu.VMEM((384, 384), BF16),
            pltpu.VMEM((256, 256), F32),
            pltpu.VMEM((16, 16, 128), F32),
            pltpu.VMEM((16, 16, 128), F32),
            dma((3,)), dma, dma, dma, dma, dma((2, 4, 2)), dma((2, 4, 2)), dma((2, 4, 2)), dma((2, 4, 2)), dma, dma,
            dma((2, 4)), dma((2, 4)), dma((2, 4)), dma((2, 4)), dma, dma,
            dma((8,)), dma((8,)), dma((2,)), dma((2,)),
        ],
        compiler_params=pltpu.CompilerParams(
            collective_id=0, has_side_effects=True, vmem_limit_bytes=48 * 1024 * 1024
        ),
    )(block_tile, sigma_owner, three_center, green, screened)


def solution(mesh):
    in_specs = (P("pair", "ri", None, None), P("pair", None, None, None), P("ri", None), P(), P())
    return jax.shard_map(
        on_device, mesh=mesh, in_specs=in_specs, out_specs=P("pair", None, None), check_vma=False
    )
```

```python
import functools

import jax
import jax.numpy as jnp
from jax import lax
from jax.experimental import pallas as pl
from jax.experimental.pallas import tpu as pltpu
from jax.sharding import PartitionSpec as P

MESH = pl.DeviceIdType.MESH
F32, BF16 = jnp.float32, jnp.bfloat16


def remote(src, dst, send_sem, recv_sem, device):
    return pltpu.make_async_remote_copy(
        src_ref=src, dst_ref=dst, send_sem=send_sem, recv_sem=recv_sem, device_id=device, device_id_type=MESH
    )


def wait_bytes(ref, sem):
    pltpu.make_async_copy(ref, ref, sem).wait()


def iota2(shape, dim):
    return lax.broadcasted_iota(jnp.int32, shape, dim)


NT = (((1,), (1,)), ((), ()))
ORDER = (0, 1, 3, 2)


def kernel(
    tiles_hbm, owner_hbm, three_hbm, green_hbm, screened_hbm, out_ref,
    tiles_ref, owner_ref, three, green, by_mu, place, stage, t_out, h_out, columns, rows, weighted, halves,
    g_wide, g_out, g_in, g_own, g_all, partials, totals,
    local_sem, a_send, a_recv, t_send, t_recv, h_send, h_recv,
    ring_send, ring_recv, sib_send, sib_recv, own_send, own_recv,
    g_send, g_recv, c_send, c_recv, f_send, f_recv,
):
    pair, ri = lax.axis_index("pair"), lax.axis_index("ri")
    z, core = pair // 2, pair % 2
    y, x = ri // 4, ri % 4
    sibling = (z * 2 + 1 - core, ri)

    def chip(step):
        return (z + step + 8) % 8

    def neighbour(step):
        return (chip(step) * 2 + core, ri)

    def plane_peer(step):
        return (ri + step) % 16

    def pair_peer(step):
        return (pair + step) % 16

    load_three = pltpu.make_async_copy(three_hbm.at[0], three, local_sem.at[0])
    load_green = pltpu.make_async_copy(green_hbm.at[0], green, local_sem.at[1])
    load_tiles = pltpu.make_async_copy(tiles_hbm, tiles_ref, local_sem.at[3])
    load_owner = pltpu.make_async_copy(owner_hbm, owner_ref, local_sem.at[4])
    mine = pl.ds(pl.multiple_of(ri * 16, 16), 16)
    row_piece = screened_hbm.at[
        pl.ds(pl.multiple_of(z * 16, 16), 16), pl.ds(pl.multiple_of(core * 1024, 1024), 1024)
    ]
    load_rows = pltpu.make_async_copy(row_piece, rows.at[z, core, mine], local_sem.at[2])
    load_three.start()
    load_tiles.start()
    load_green.start()
    load_rows.start()
    load_owner.start()
    barrier = pltpu.get_barrier_semaphore()

    @pl.loop(1, 16)
    def _(step):
        pl.semaphore_signal(barrier, inc=1, device_id=(pair, plane_peer(step)), device_id_type=MESH)
        pl.semaphore_signal(barrier, inc=1, device_id=(pair_peer(step), ri), device_id_type=MESH)

    first, second = iota2((256, 256), 0), iota2((256, 256), 1)
    swap = ((first % 16) * 16 + first // 16 == second).astype(BF16)
    spot, lane = iota2((768, 384), 0), iota2((768, 384), 1)
    wanted = (spot // 48) * 24 + spot % 24 == lane
    for odd in range(2):
        place[odd] = (wanted & ((spot % 48) // 24 == odd)).astype(BF16)
    load_three.wait()

    @pl.loop(0, 8)
    def _(chunk):
        at = pl.ds(pl.multiple_of(chunk * 16, 16), 16)
        block = three[at].reshape(256, 384)
        by_mu[:, at] = jnp.dot(swap, block, preferred_element_type=F32).astype(BF16).reshape(16, 16, 384)

    def arrange(out):
        @pl.loop(0, 8)
        def _(two):
            block = lax.dot_general(place[0], by_mu[2 * two], NT, preferred_element_type=F32)
            block += lax.dot_general(place[1], by_mu[2 * two + 1], NT, preferred_element_type=F32)
            out[:, pl.ds(pl.multiple_of(two * 48, 16), 48)] = block.astype(BF16).reshape(16, 48, 128)

    arrange(stage)

    load_green.wait()
    load_tiles.wait()
    load_owner.wait()
    green_rows = pl.ds(pl.multiple_of(y * 16, 16), 16)

    @pl.loop(0, 16)
    def _(region):
        for j in range(6):
            g_wide[j, region] = green[tiles_ref[j, region], green_rows, :]

    source, target = iota2((64, 128), 0), iota2((64, 128), 1)
    picked = jnp.zeros((256, 128), F32)
    for j in range(6):
        spots = ((target // 16 == j) & (source == x * 16 + target % 16)).astype(BF16)
        picked += jnp.dot(g_wide[j].reshape(256, 64), spots, preferred_element_type=F32)
    g_out[...] = picked.astype(BF16).reshape(16, 16, 128)
    g_in[pair] = g_out[pair]
    load_rows.wait()
    pl.semaphore_wait(barrier, 30)

    for q in ORDER:
        for dx in range(4):
            if q or dx:
                peer = ((y + 4 - q) % 4) * 4 + (x + dx) % 4
                remote(row_piece, rows.at[z, core, mine], a_send, a_recv.at[q], (pair, peer)).start()

    @pl.loop(1, 16)
    def _(step):
        peer = pair_peer(step)
        remote(g_out.at[peer], g_in.at[pair], g_send, g_recv, (peer, ri)).start()

    own_columns = pl.ds(pl.multiple_of(ri * 128, 128), 128)
    eye = (iota2((128, 128), 0) == iota2((128, 128), 1)).astype(BF16)

    @pl.loop(0, 16)
    def _(peer):
        t_out[peer] = lax.dot_general(eye, stage[peer], NT, preferred_element_type=F32).astype(BF16)

    def part_of(step, which, q, count=64):
        return rows.at[chip(step), which, pl.ds(pl.multiple_of(((y + q) % 4) * 64, 64), count)]

    def ring(way, step, q):
        i = (1 - way) // 2
        ref = part_of(-way * (step - 1), core, q)
        return remote(ref, ref, ring_send.at[i, step - 1, q], ring_recv.at[i, step - 1, q], neighbour(way))

    def side(way, step, q):
        i = (1 - way) // 2
        ref = part_of(-way * step, core, q)
        return remote(ref, ref, sib_send.at[i, step - 1, q], sib_recv.at[i, step - 1, q], sibling)

    def own_side(q):
        ref = part_of(0, core, q)
        return remote(ref, ref, own_send.at[q], own_recv.at[q], sibling)

    def parts_at(way, step):
        if step < 4:
            return ORDER
        return ORDER[0:2] if way == 1 else ORDER[2:4]

    def begin(q):
        wait_bytes(part_of(0, core, q, 64 if q else 48), a_recv.at[q])
        for way in (1, -1):
            ring(way, 1, q).start()
        own_side(q).start()

    begin(ORDER[0])

    wait_bytes(g_in.at[pl.ds(0, 15)], g_recv)
    for k in range(6):
        g_own[k] = g_in[tiles_ref[k, pair]]
    g_place = g_all.at[:, y, :, pl.ds(pl.multiple_of(x * 128, 128), 128)]

    def share(step):
        return remote(g_own, g_place, c_send.at[step], c_recv.at[step], (pair, plane_peer(step)))

    @pl.loop(1, 16)
    def _(step):
        share(step).start()

    g_all[:, y, :, pl.ds(pl.multiple_of(x * 128, 128), 128)] = g_own[...]

    @pl.loop(1, 16)
    def _(step):
        peer = plane_peer(step)
        remote(t_out.at[peer], columns.at[own_columns], t_send, t_recv, (pair, peer)).start()

    columns[own_columns, :] = t_out[ri]
    for q in ORDER[1:]:
        begin(q)

    def serve(step):
        for q in ORDER:
            for way in (1, -1):
                if q in parts_at(way, step):
                    wait_bytes(part_of(-way * step, core, q), ring_recv.at[(1 - way) // 2, step - 1, q])
                    if step < 4 and q in parts_at(way, step + 1):
                        ring(way, step + 1, q).start()
                    side(way, step, q).start()

    def sides_in(way, step):
        for q in parts_at(way, step):
            wait_bytes(part_of(-way * step, 1 - core, q), sib_recv.at[(1 - way) // 2, step - 1, q])

    def process(step):
        piece = chip(step)
        total = jnp.dot(rows[piece, 0], columns[0:1024], preferred_element_type=F32)
        total += jnp.dot(rows[piece, 1], columns[1024:2048], preferred_element_type=F32)
        at = pl.ds(pl.multiple_of(piece * 16, 16), 16)
        weighted[:, at] = total.astype(BF16).reshape(16, 16, 384)

    serve(1)

    @pl.loop(1, 16)
    def _(step):
        share(step).wait_recv()

    source, target = iota2((512, 384), 0), iota2((512, 384), 1)
    order = (
        (source // 128 == (target // 16) % 4) & ((source % 128) // 16 == target // 64) & (source % 16 == target % 16)
    ).astype(BF16)
    coupling = jnp.dot(g_all[...].reshape(384, 512), order, preferred_element_type=F32).astype(BF16)
    for odd in range(2):
        place[odd] = lax.dot_general(place[odd], coupling, NT, preferred_element_type=F32).astype(BF16)
    arrange(h_out)
    own_lanes = pl.ds(pl.multiple_of(ri * 128, 128), 128)

    @pl.loop(1, 16)
    def _(step):
        peer = plane_peer(step)
        remote(h_out.at[peer], halves.at[:, own_lanes], h_send, h_recv, (pair, peer)).start()

    halves[:, own_lanes] = h_out[ri]

    serve(2)
    wait_bytes(columns.at[pl.ds(0, 1920)], t_recv)
    for q in ORDER:
        wait_bytes(part_of(0, 1 - core, q), own_recv.at[q])
    process(0)
    for step in (1, 2):
        for way in (1, -1):
            sides_in(way, step)
            process(-way * step)
    serve(3)
    for way in (1, -1):
        sides_in(way, 3)
        process(-3 * way)
    serve(4)
    for way in (1, -1):
        sides_in(way, 4)
    process(4)
    wait_bytes(halves.at[:, pl.ds(0, 1920)], h_recv)
    gram = jnp.dot(halves[...], weighted[...].reshape(2048, 384), preferred_element_type=F32)

    masked = jnp.where(iota2((384, 384), 0) % 24 == iota2((384, 384), 1) % 24, gram, 0.0)
    fold = (iota2((16, 384), 1) // 24 == iota2((16, 384), 0)).astype(F32)
    folded = jnp.dot(fold, masked, preferred_element_type=F32, precision=lax.Precision.HIGHEST)
    spread = (iota2((384, 128), 0) // 24 == iota2((384, 128), 1) % 16).astype(F32)
    wide = jnp.dot(folded, spread, preferred_element_type=F32, precision=lax.Precision.HIGHEST)
    keep = iota2((16, 128), 1) // 16 == iota2((16, 128), 0) % 8
    partials[ri] = jnp.sum(jnp.where(keep, wide, 0.0).reshape(2, 8, 128), axis=1)

    @pl.loop(1, 16)
    def _(step):
        remote(partials.at[ri], partials.at[ri], f_send.at[0], f_recv.at[0], (pair, plane_peer(step))).start()

    wait_bytes(partials.at[pl.ds(0, 15)], f_recv.at[0])
    totals[pair] = -jnp.sum(partials[...], axis=0)

    @pl.loop(1, 16)
    def _(step):
        remote(totals.at[pair], totals.at[pair], f_send.at[1], f_recv.at[1], (pair_peer(step), ri)).start()

    wait_bytes(rows.at[z, core, pl.ds(0, 240)], a_send)
    wait_bytes(columns.at[pl.ds(0, 1920)], t_send)
    wait_bytes(halves.at[:, pl.ds(0, 1920)], h_send)
    wait_bytes(g_in.at[pl.ds(0, 15)], g_send)
    for q in ORDER:
        own_side(q).wait_send()
    for step in (1, 2, 3, 4):
        for way in (1, -1):
            for q in parts_at(way, step):
                ring(way, step, q).wait_send()
                side(way, step, q).wait_send()

    @pl.loop(1, 16)
    def _(step):
        share(step).wait_send()

    wait_bytes(partials.at[pl.ds(0, 15)], f_send.at[0])
    wait_bytes(totals.at[pl.ds(0, 15)], f_send.at[1])
    wait_bytes(totals.at[pl.ds(0, 15)], f_recv.at[1])
    result = jnp.zeros((2, 128), F32)
    for region in range(16):
        result += jnp.where(owner_ref[region] == pair, totals[region], 0.0)
    again = jnp.broadcast_to(result[:, None, :], (2, 8, 128)).reshape(16, 128)
    narrow = (iota2((128, 16), 0) % 16 == iota2((128, 16), 1)).astype(F32)
    out_ref[0] = jnp.dot(
        jnp.where(keep, again, 0.0), narrow, preferred_element_type=F32, precision=lax.Precision.HIGHEST
    )


def on_device(three_center, green, screened, block_tile, sigma_owner):
    dma = pltpu.SemaphoreType.DMA
    return pl.pallas_call(
        kernel,
        out_shape=jax.ShapeDtypeStruct((1, 16, 16), F32),
        in_specs=[pl.BlockSpec(memory_space=pltpu.HBM)] * 5,
        out_specs=pl.BlockSpec(memory_space=pltpu.VMEM),
        scratch_shapes=[
            pltpu.SMEM((6, 16), jnp.int32),
            pltpu.SMEM((16,), jnp.int32),
            pltpu.VMEM((128, 16, 384), BF16),
            pltpu.VMEM((16, 64, 64), BF16),
            pltpu.VMEM((16, 128, 384), BF16),
            pltpu.VMEM((2, 768, 384), BF16),
            pltpu.VMEM((16, 384, 128), BF16),
            pltpu.VMEM((16, 128, 384), BF16),
            pltpu.VMEM((16, 384, 128), BF16),
            pltpu.VMEM((2048, 384), BF16),
            pltpu.VMEM((8, 2, 256, 1024), BF16),
            pltpu.VMEM((16, 128, 384), BF16),
            pltpu.VMEM((384, 2048), BF16),
            pltpu.VMEM((6, 16, 16, 64), BF16),
            pltpu.VMEM((16, 16, 128), BF16),
            pltpu.VMEM((16, 16, 128), BF16),
            pltpu.VMEM((6, 16, 128), BF16),
            pltpu.VMEM((6, 4, 16, 512), BF16),
            pltpu.VMEM((16, 2, 128), F32),
            pltpu.VMEM((16, 2, 128), F32),
            dma((5,)), dma, dma((4,)), dma, dma, dma, dma,
            dma((2, 4, 4)), dma((2, 4, 4)), dma((2, 4, 4)), dma((2, 4, 4)), dma((4,)), dma((4,)),
            dma, dma, dma((16,)), dma((16,)), dma((2,)), dma((2,)),
        ],
        compiler_params=pltpu.CompilerParams(
            collective_id=0, has_side_effects=True, vmem_limit_bytes=60 * 1024 * 1024
        ),
    )(block_tile.T, sigma_owner, three_center, green, screened)


def solution(mesh):
    in_specs = (P("pair", "ri", None, None), P("pair", None, None, None), P("ri", None), P(), P())
    return jax.shard_map(
        on_device, mesh=mesh, in_specs=in_specs, out_specs=P("pair", None, None), check_vma=False
    )
```

```python
import functools

import jax
import jax.numpy as jnp
from jax import lax
from jax.experimental import pallas as pl
from jax.experimental.pallas import tpu as pltpu
from jax.sharding import PartitionSpec as P

MESH = pl.DeviceIdType.MESH
F32, BF16 = jnp.float32, jnp.bfloat16


def remote(src, dst, send_sem, recv_sem, device):
    return pltpu.make_async_remote_copy(
        src_ref=src, dst_ref=dst, send_sem=send_sem, recv_sem=recv_sem, device_id=device, device_id_type=MESH
    )


def wait_bytes(ref, sem):
    pltpu.make_async_copy(ref, ref, sem).wait()


def iota2(shape, dim):
    return lax.broadcasted_iota(jnp.int32, shape, dim)


NT = (((1,), (1,)), ((), ()))
ORDER = (0, 1, 3, 2)


def kernel(
    tiles_hbm, owner_hbm, three_hbm, green_hbm, screened_hbm, out_ref,
    tiles_ref, owner_ref, three, green, by_mu, left, stage, t_out, h_out, columns, rows, weighted, halves,
    g_wide, g_out, g_in, g_own, g_all, partials, totals,
    local_sem, a_send, a_recv, t_send, t_recv, h_send, h_recv,
    ring_send, ring_recv, sib_send, sib_recv, own_send, own_recv,
    g_send, g_recv, c_send, c_recv, f_send, f_recv,
):
    pair, ri = lax.axis_index("pair"), lax.axis_index("ri")
    z, core = pair // 2, pair % 2
    y, x = ri // 4, ri % 4
    sibling = (z * 2 + 1 - core, ri)

    def chip(step):
        return (z + step + 8) % 8

    def neighbour(step):
        return (chip(step) * 2 + core, ri)

    def plane_peer(step):
        return (ri + step) % 16

    def pair_peer(step):
        return (pair + step) % 16

    load_three = pltpu.make_async_copy(three_hbm.at[0], three, local_sem.at[0])
    load_green = pltpu.make_async_copy(green_hbm.at[0], green, local_sem.at[1])
    load_tiles = pltpu.make_async_copy(tiles_hbm, tiles_ref, local_sem.at[3])
    load_owner = pltpu.make_async_copy(owner_hbm, owner_ref, local_sem.at[4])
    mine = pl.ds(pl.multiple_of(ri * 16, 16), 16)
    row_piece = screened_hbm.at[
        pl.ds(pl.multiple_of(z * 16, 16), 16), pl.ds(pl.multiple_of(core * 1024, 1024), 1024)
    ]
    load_rows = pltpu.make_async_copy(row_piece, rows.at[z, core, mine], local_sem.at[2])
    load_three.start()
    load_tiles.start()
    load_green.start()
    load_rows.start()
    load_owner.start()
    barrier = pltpu.get_barrier_semaphore()

    @pl.loop(1, 16)
    def _(step):
        pl.semaphore_signal(barrier, inc=1, device_id=(pair, plane_peer(step)), device_id_type=MESH)
        pl.semaphore_signal(barrier, inc=1, device_id=(pair_peer(step), ri), device_id_type=MESH)

    load_green.wait()
    load_tiles.wait()
    load_owner.wait()
    green_rows = pl.ds(pl.multiple_of(y * 16, 16), 16)

    @pl.loop(0, 16)
    def _(region):
        for j in range(6):
            g_wide[j, region] = green[tiles_ref[j, region], green_rows, :]

    source, target = iota2((64, 384), 0), iota2((64, 384), 1)
    picked = jnp.zeros((256, 384), F32)
    for j in range(6):
        spots = (target == source + j * 64).astype(BF16)
        picked += jnp.dot(g_wide[j].reshape(256, 64), spots, preferred_element_type=F32)
    g_out[...] = picked.astype(BF16).reshape(16, 16, 384)
    g_in[pair] = g_out[pair]

    first, second = iota2((256, 256), 0), iota2((256, 256), 1)
    swap = ((first % 16) * 16 + first // 16 == second).astype(BF16)
    load_three.wait()

    for chunk in range(8):
        at = pl.ds(chunk * 16, 16)
        block = three[at].reshape(256, 384)
        by_mu[:, at] = jnp.dot(swap, block, preferred_element_type=F32).astype(BF16).reshape(16, 16, 384)

    def arrange(out):
        for two in range(8):
            pieces = by_mu[2 * two:2 * two + 2].reshape(256, 384)
            block = lax.dot_general(left[...], pieces, NT, preferred_element_type=F32)
            both = [block[:, :128].reshape(16, 24, 128), block[:, 128:].reshape(16, 24, 128)]
            out[:, two * 48:two * 48 + 48] = jnp.concatenate(both, axis=1).astype(BF16)

    unit = (iota2((384, 384), 0) == iota2((384, 384), 1)).astype(BF16)
    left[...] = unit
    arrange(stage)
    load_rows.wait()
    pl.semaphore_wait(barrier, 30)

    def offer(q):
        for dx in range(4):
            if q or dx:
                peer = ((y + 4 - q) % 4) * 4 + (x + dx) % 4
                remote(row_piece, rows.at[z, core, mine], a_send, a_recv.at[q], (pair, peer)).start()

    offer(ORDER[0])

    @pl.loop(1, 16)
    def _(step):
        peer = pair_peer(step)
        remote(g_out.at[peer], g_in.at[pair], g_send, g_recv, (peer, ri)).start()

    for q in ORDER[1:]:
        offer(q)

    own_columns = pl.ds(pl.multiple_of(ri * 128, 128), 128)
    eye = (iota2((128, 128), 0) == iota2((128, 128), 1)).astype(BF16)

    for peer in range(16):
        t_out[peer] = lax.dot_general(eye, stage[peer], NT, preferred_element_type=F32).astype(BF16)

    def part_of(step, which, q, count=64):
        return rows.at[chip(step), which, pl.ds(pl.multiple_of(((y + q) % 4) * 64, 64), count)]

    def ring(way, step, q):
        i = (1 - way) // 2
        ref = part_of(-way * (step - 1), core, q)
        return remote(ref, ref, ring_send.at[i, step - 1, q], ring_recv.at[i, step - 1, q], neighbour(way))

    def side(way, step, q):
        i = (1 - way) // 2
        ref = part_of(-way * step, core, q)
        return remote(ref, ref, sib_send.at[i, step - 1, q], sib_recv.at[i, step - 1, q], sibling)

    def own_side(q):
        ref = part_of(0, core, q)
        return remote(ref, ref, own_send.at[q], own_recv.at[q], sibling)

    def parts_at(way, step):
        if step < 4:
            return ORDER
        return ORDER[0:2] if way == 1 else ORDER[2:4]

    def begin(q):
        wait_bytes(part_of(0, core, q, 64 if q else 48), a_recv.at[q])
        for way in (1, -1):
            ring(way, 1, q).start()
        own_side(q).start()

    def send_three(step):
        peer = plane_peer(step)
        remote(t_out.at[peer], columns.at[own_columns], t_send, t_recv, (pair, peer)).start()

    begin(ORDER[0])
    pl.loop(1, 8)(send_three)

    wait_bytes(g_in.at[pl.ds(0, 15)], g_recv)
    for k in range(6):
        g_own[k] = g_in[tiles_ref[k, pair]]

    def share(step):
        peer = ((y + step) % 4) * 4 + x
        return remote(g_own, g_all.at[:, y], c_send.at[step], c_recv.at[step], (pair, peer))

    for step in (1, 3, 2):
        share(step).start()
    g_all[:, y] = g_own[...]
    pl.loop(8, 16)(send_three)
    columns[own_columns, :] = t_out[ri]
    for q in ORDER[1:]:
        begin(q)

    def serve(step):
        for q in ORDER:
            for way in (1, -1):
                if q in parts_at(way, step):
                    wait_bytes(part_of(-way * step, core, q), ring_recv.at[(1 - way) // 2, step - 1, q])
                    if step < 4 and q in parts_at(way, step + 1):
                        ring(way, step + 1, q).start()
                    side(way, step, q).start()

    def sides_in(way, step):
        for q in parts_at(way, step):
            wait_bytes(part_of(-way * step, 1 - core, q), sib_recv.at[(1 - way) // 2, step - 1, q])

    def process(step):
        piece = chip(step)
        total = jnp.dot(rows[piece, 0], columns[0:1024], preferred_element_type=F32)
        total += jnp.dot(rows[piece, 1], columns[1024:2048], preferred_element_type=F32)
        at = pl.ds(pl.multiple_of(piece * 16, 16), 16)
        weighted[:, at] = total.astype(BF16).reshape(16, 16, 384)

    serve(1)

    for step in (1, 3, 2):
        share(step).wait_recv()
    left[...] = lax.dot_general(unit, g_all[...].reshape(384, 384), NT, preferred_element_type=F32).astype(BF16)
    arrange(h_out)
    own_lanes = pl.ds(pl.multiple_of(ri * 128, 128), 128)

    @pl.loop(1, 16)
    def _(step):
        peer = plane_peer(step)
        remote(h_out.at[peer], halves.at[:, own_lanes], h_send, h_recv, (pair, peer)).start()

    halves[:, own_lanes] = h_out[ri]

    serve(2)
    wait_bytes(columns.at[pl.ds(0, 1920)], t_recv)
    for q in ORDER:
        wait_bytes(part_of(0, 1 - core, q), own_recv.at[q])
    process(0)
    for step in (1, 2):
        for way in (1, -1):
            sides_in(way, step)
            process(-way * step)
    serve(3)
    for way in (1, -1):
        sides_in(way, 3)
        process(-3 * way)
    serve(4)
    for way in (1, -1):
        sides_in(way, 4)
    process(4)
    wait_bytes(halves.at[:, pl.ds(0, 1920)], h_recv)
    gram = jnp.dot(halves[...], weighted[...].reshape(2048, 384), preferred_element_type=F32)

    masked = jnp.where(iota2((384, 384), 0) % 24 == iota2((384, 384), 1) % 24, gram, 0.0)
    folded = jnp.sum(masked.reshape(16, 24, 384), axis=1)
    spread = (iota2((384, 128), 0) // 24 == iota2((384, 128), 1) % 16).astype(F32)
    wide = jnp.dot(folded, spread, preferred_element_type=F32, precision=lax.Precision.HIGHEST)
    keep = iota2((16, 128), 1) // 16 == iota2((16, 128), 0) % 8
    partials[ri] = jnp.sum(jnp.where(keep, wide, 0.0).reshape(2, 8, 128), axis=1)

    @pl.loop(1, 16)
    def _(step):
        remote(partials.at[ri], partials.at[ri], f_send.at[0], f_recv.at[0], (pair, plane_peer(step))).start()

    wait_bytes(partials.at[pl.ds(0, 15)], f_recv.at[0])
    totals[pair] = -jnp.sum(partials[...], axis=0)

    @pl.loop(1, 16)
    def _(step):
        remote(totals.at[pair], totals.at[pair], f_send.at[1], f_recv.at[1], (pair_peer(step), ri)).start()

    wait_bytes(rows.at[z, core, pl.ds(0, 240)], a_send)
    wait_bytes(columns.at[pl.ds(0, 1920)], t_send)
    wait_bytes(halves.at[:, pl.ds(0, 1920)], h_send)
    wait_bytes(g_in.at[pl.ds(0, 15)], g_send)
    for q in ORDER:
        own_side(q).wait_send()
    for step in (1, 2, 3, 4):
        for way in (1, -1):
            for q in parts_at(way, step):
                ring(way, step, q).wait_send()
                side(way, step, q).wait_send()

    for step in (1, 3, 2):
        share(step).wait_send()
    wait_bytes(partials.at[pl.ds(0, 15)], f_send.at[0])
    wait_bytes(totals.at[pl.ds(0, 15)], f_send.at[1])
    wait_bytes(totals.at[pl.ds(0, 15)], f_recv.at[1])
    result = jnp.zeros((2, 128), F32)
    for region in range(16):
        result += jnp.where(owner_ref[region] == pair, totals[region], 0.0)
    again = jnp.broadcast_to(result[:, None, :], (2, 8, 128)).reshape(16, 128)
    narrow = (iota2((128, 16), 0) % 16 == iota2((128, 16), 1)).astype(F32)
    out_ref[0] = jnp.dot(
        jnp.where(keep, again, 0.0), narrow, preferred_element_type=F32, precision=lax.Precision.HIGHEST
    )


def on_device(three_center, green, screened, block_tile, sigma_owner):
    dma = pltpu.SemaphoreType.DMA
    return pl.pallas_call(
        kernel,
        out_shape=jax.ShapeDtypeStruct((1, 16, 16), F32),
        in_specs=[pl.BlockSpec(memory_space=pltpu.HBM)] * 5,
        out_specs=pl.BlockSpec(memory_space=pltpu.VMEM),
        scratch_shapes=[
            pltpu.SMEM((6, 16), jnp.int32),
            pltpu.SMEM((16,), jnp.int32),
            pltpu.VMEM((128, 16, 384), BF16),
            pltpu.VMEM((16, 64, 64), BF16),
            pltpu.VMEM((16, 128, 384), BF16),
            pltpu.VMEM((384, 384), BF16),
            pltpu.VMEM((16, 384, 128), BF16),
            pltpu.VMEM((16, 128, 384), BF16),
            pltpu.VMEM((16, 384, 128), BF16),
            pltpu.VMEM((2048, 384), BF16),
            pltpu.VMEM((8, 2, 256, 1024), BF16),
            pltpu.VMEM((16, 128, 384), BF16),
            pltpu.VMEM((384, 2048), BF16),
            pltpu.VMEM((6, 16, 16, 64), BF16),
            pltpu.VMEM((16, 16, 384), BF16),
            pltpu.VMEM((16, 16, 384), BF16),
            pltpu.VMEM((6, 16, 384), BF16),
            pltpu.VMEM((6, 4, 16, 384), BF16),
            pltpu.VMEM((16, 2, 128), F32),
            pltpu.VMEM((16, 2, 128), F32),
            dma((5,)), dma, dma((4,)), dma, dma, dma, dma,
            dma((2, 4, 4)), dma((2, 4, 4)), dma((2, 4, 4)), dma((2, 4, 4)), dma((4,)), dma((4,)),
            dma, dma, dma((4,)), dma((4,)), dma((2,)), dma((2,)),
        ],
        compiler_params=pltpu.CompilerParams(
            collective_id=0, has_side_effects=True, vmem_limit_bytes=60 * 1024 * 1024
        ),
    )(block_tile.T, sigma_owner, three_center, green, screened)


def solution(mesh):
    in_specs = (P("pair", "ri", None, None), P("pair", None, None, None), P("ri", None), P(), P())
    return jax.shard_map(
        on_device, mesh=mesh, in_specs=in_specs, out_specs=P("pair", None, None), check_vma=False
    )
```

```python
import functools

import jax
import jax.numpy as jnp
from jax import lax
from jax.experimental import pallas as pl
from jax.experimental.pallas import tpu as pltpu
from jax.sharding import PartitionSpec as P

MESH = pl.DeviceIdType.MESH
F32, BF16 = jnp.float32, jnp.bfloat16


def remote(src, dst, send_sem, recv_sem, device):
    return pltpu.make_async_remote_copy(
        src_ref=src, dst_ref=dst, send_sem=send_sem, recv_sem=recv_sem, device_id=device, device_id_type=MESH
    )


def wait_bytes(ref, sem):
    pltpu.make_async_copy(ref, ref, sem).wait()


def iota2(shape, dim):
    return lax.broadcasted_iota(jnp.int32, shape, dim)


NT = (((1,), (1,)), ((), ()))
ORDER = (0, 1, 3, 2)


def kernel(
    tiles_hbm, owner_hbm, three_hbm, green_hbm, screened_hbm, out_ref,
    tiles_ref, owner_ref, three, green, by_mu, left, stage, t_out, h_out, columns, rows, weighted, halves,
    g_wide, g_out, g_in, g_own, g_all, partials, totals,
    local_sem, a_send, a_recv, t_send, t_recv, h_send, h_recv,
    ring_send, ring_recv, sib_send, sib_recv, own_send, own_recv,
    g_send, g_recv, c_send, c_recv, f_send, f_recv,
):
    pair, ri = lax.axis_index("pair"), lax.axis_index("ri")
    z, core = pair // 2, pair % 2
    y, x = ri // 4, ri % 4
    sibling = (z * 2 + 1 - core, ri)

    def chip(step):
        return (z + step + 8) % 8

    def neighbour(step):
        return (chip(step) * 2 + core, ri)

    def plane_peer(step):
        return (ri + step) % 16

    def pair_peer(step):
        return (pair + step) % 16

    load_three = pltpu.make_async_copy(three_hbm.at[0], three, local_sem.at[0])
    load_green = pltpu.make_async_copy(green_hbm.at[0], green, local_sem.at[1])
    load_tiles = pltpu.make_async_copy(tiles_hbm, tiles_ref, local_sem.at[3])
    load_owner = pltpu.make_async_copy(owner_hbm, owner_ref, local_sem.at[4])
    mine = pl.ds(pl.multiple_of(ri * 16, 16), 16)
    row_piece = screened_hbm.at[
        pl.ds(pl.multiple_of(z * 16, 16), 16), pl.ds(pl.multiple_of(core * 1024, 1024), 1024)
    ]
    load_rows = pltpu.make_async_copy(row_piece, rows.at[z, core, mine], local_sem.at[2])
    load_three.start()
    load_tiles.start()
    load_green.start()
    load_rows.start()
    load_owner.start()
    barrier = pltpu.get_barrier_semaphore()

    @pl.loop(1, 16)
    def _(step):
        pl.semaphore_signal(barrier, inc=1, device_id=(pair, plane_peer(step)), device_id_type=MESH)
        pl.semaphore_signal(barrier, inc=1, device_id=(pair_peer(step), ri), device_id_type=MESH)

    load_green.wait()
    load_tiles.wait()
    load_owner.wait()
    green_rows = pl.ds(pl.multiple_of(y * 16, 16), 16)

    @pl.loop(0, 16)
    def _(region):
        for j in range(6):
            g_wide[j, region] = green[tiles_ref[j, region], green_rows, :]

    source, target = iota2((64, 384), 0), iota2((64, 384), 1)
    picked = jnp.zeros((256, 384), F32)
    for j in range(6):
        spots = (target == source + j * 64).astype(BF16)
        picked += jnp.dot(g_wide[j].reshape(256, 64), spots, preferred_element_type=F32)
    g_out[...] = picked.astype(BF16).reshape(16, 16, 384)
    g_in[pair] = g_out[pair]

    load_rows.wait()
    pl.semaphore_wait(barrier, 30)

    def offer(q):
        for dx in range(4):
            if q or dx:
                peer = ((y + 4 - q) % 4) * 4 + (x + dx) % 4
                remote(row_piece, rows.at[z, core, mine], a_send, a_recv.at[q], (pair, peer)).start()

    offer(ORDER[0])

    @pl.loop(1, 16)
    def _(step):
        peer = pair_peer(step)
        remote(g_out.at[peer], g_in.at[pair], g_send, g_recv, (peer, ri)).start()

    for q in ORDER[1:]:
        offer(q)

    first, second = iota2((256, 256), 0), iota2((256, 256), 1)
    swap = ((first % 16) * 16 + first // 16 == second).astype(BF16)
    load_three.wait()

    for chunk in range(8):
        at = pl.ds(chunk * 16, 16)
        block = three[at].reshape(256, 384)
        by_mu[:, at] = jnp.dot(swap, block, preferred_element_type=F32).astype(BF16).reshape(16, 16, 384)

    def arrange(out):
        for two in range(8):
            pieces = by_mu[2 * two:2 * two + 2].reshape(256, 384)
            block = lax.dot_general(left[...], pieces, NT, preferred_element_type=F32)
            both = [block[:, :128].reshape(16, 24, 128), block[:, 128:].reshape(16, 24, 128)]
            out[:, two * 48:two * 48 + 48] = jnp.concatenate(both, axis=1).astype(BF16)

    unit = (iota2((384, 384), 0) == iota2((384, 384), 1)).astype(BF16)
    left[...] = unit
    arrange(stage)
    own_columns = pl.ds(pl.multiple_of(ri * 128, 128), 128)
    eye = (iota2((128, 128), 0) == iota2((128, 128), 1)).astype(BF16)

    for peer in range(16):
        t_out[peer] = lax.dot_general(eye, stage[peer], NT, preferred_element_type=F32).astype(BF16)

    def part_of(step, which, q, count=64):
        return rows.at[chip(step), which, pl.ds(pl.multiple_of(((y + q) % 4) * 64, 64), count)]

    def ring(way, step, q):
        i = (1 - way) // 2
        ref = part_of(-way * (step - 1), core, q)
        return remote(ref, ref, ring_send.at[i, step - 1, q], ring_recv.at[i, step - 1, q], neighbour(way))

    def side(way, step, q):
        i = (1 - way) // 2
        ref = part_of(-way * step, core, q)
        return remote(ref, ref, sib_send.at[i, step - 1, q], sib_recv.at[i, step - 1, q], sibling)

    def own_side(q):
        ref = part_of(0, core, q)
        return remote(ref, ref, own_send.at[q], own_recv.at[q], sibling)

    def parts_at(way, step):
        if step < 4:
            return ORDER
        return ORDER[0:2] if way == 1 else ORDER[2:4]

    def begin(q):
        wait_bytes(part_of(0, core, q, 64 if q else 48), a_recv.at[q])
        for way in (1, -1):
            ring(way, 1, q).start()
        own_side(q).start()

    def send_three(step):
        peer = plane_peer(step)
        remote(t_out.at[peer], columns.at[own_columns], t_send, t_recv, (pair, peer)).start()

    begin(ORDER[0])
    pl.loop(1, 8)(send_three)

    wait_bytes(g_in.at[pl.ds(0, 15)], g_recv)
    for k in range(6):
        g_own[k] = g_in[tiles_ref[k, pair]]

    def share(step):
        peer = ((y + step) % 4) * 4 + x
        return remote(g_own, g_all.at[:, y], c_send.at[step], c_recv.at[step], (pair, peer))

    for step in (1, 3, 2):
        share(step).start()
    g_all[:, y] = g_own[...]
    pl.loop(8, 16)(send_three)
    columns[own_columns, :] = t_out[ri]
    for q in ORDER[1:]:
        begin(q)

    def serve(step):
        for q in ORDER:
            for way in (1, -1):
                if q in parts_at(way, step):
                    wait_bytes(part_of(-way * step, core, q), ring_recv.at[(1 - way) // 2, step - 1, q])
                    if step < 4 and q in parts_at(way, step + 1):
                        ring(way, step + 1, q).start()
                    side(way, step, q).start()

    def sides_in(way, step):
        for q in parts_at(way, step):
            wait_bytes(part_of(-way * step, 1 - core, q), sib_recv.at[(1 - way) // 2, step - 1, q])

    def process(step):
        piece = chip(step)
        total = jnp.dot(rows[piece, 0], columns[0:1024], preferred_element_type=F32)
        total += jnp.dot(rows[piece, 1], columns[1024:2048], preferred_element_type=F32)
        at = pl.ds(pl.multiple_of(piece * 16, 16), 16)
        weighted[:, at] = total.astype(BF16).reshape(16, 16, 384)

    serve(1)

    for step in (1, 3, 2):
        share(step).wait_recv()
    left[...] = lax.dot_general(unit, g_all[...].reshape(384, 384), NT, preferred_element_type=F32).astype(BF16)
    arrange(h_out)
    own_lanes = pl.ds(pl.multiple_of(ri * 128, 128), 128)

    @pl.loop(1, 16)
    def _(step):
        peer = plane_peer(step)
        remote(h_out.at[peer], halves.at[:, own_lanes], h_send, h_recv, (pair, peer)).start()

    halves[:, own_lanes] = h_out[ri]

    serve(2)
    wait_bytes(columns.at[pl.ds(0, 1920)], t_recv)
    for q in ORDER:
        wait_bytes(part_of(0, 1 - core, q), own_recv.at[q])
    process(0)
    for step in (1, 2):
        for way in (1, -1):
            sides_in(way, step)
            process(-way * step)
    serve(3)
    for way in (1, -1):
        sides_in(way, 3)
        process(-3 * way)
    serve(4)
    for way in (1, -1):
        sides_in(way, 4)
    process(4)
    wait_bytes(halves.at[:, pl.ds(0, 1920)], h_recv)
    gram = jnp.dot(halves[...], weighted[...].reshape(2048, 384), preferred_element_type=F32)

    masked = jnp.where(iota2((384, 384), 0) % 24 == iota2((384, 384), 1) % 24, gram, 0.0)
    folded = jnp.sum(masked.reshape(16, 24, 384), axis=1)
    spread = (iota2((384, 128), 0) // 24 == iota2((384, 128), 1) % 16).astype(F32)
    wide = jnp.dot(folded, spread, preferred_element_type=F32, precision=lax.Precision.HIGHEST)
    keep = iota2((16, 128), 1) // 16 == iota2((16, 128), 0) % 8
    partials[ri] = jnp.sum(jnp.where(keep, wide, 0.0).reshape(2, 8, 128), axis=1)

    @pl.loop(1, 16)
    def _(step):
        remote(partials.at[ri], partials.at[ri], f_send.at[0], f_recv.at[0], (pair, plane_peer(step))).start()

    wait_bytes(partials.at[pl.ds(0, 15)], f_recv.at[0])
    totals[pair] = -jnp.sum(partials[...], axis=0)

    @pl.loop(1, 16)
    def _(step):
        remote(totals.at[pair], totals.at[pair], f_send.at[1], f_recv.at[1], (pair_peer(step), ri)).start()

    wait_bytes(rows.at[z, core, pl.ds(0, 240)], a_send)
    wait_bytes(columns.at[pl.ds(0, 1920)], t_send)
    wait_bytes(halves.at[:, pl.ds(0, 1920)], h_send)
    wait_bytes(g_in.at[pl.ds(0, 15)], g_send)
    for q in ORDER:
        own_side(q).wait_send()
    for step in (1, 2, 3, 4):
        for way in (1, -1):
            for q in parts_at(way, step):
                ring(way, step, q).wait_send()
                side(way, step, q).wait_send()

    for step in (1, 3, 2):
        share(step).wait_send()
    wait_bytes(partials.at[pl.ds(0, 15)], f_send.at[0])
    wait_bytes(totals.at[pl.ds(0, 15)], f_send.at[1])
    wait_bytes(totals.at[pl.ds(0, 15)], f_recv.at[1])
    result = jnp.zeros((2, 128), F32)
    for region in range(16):
        result += jnp.where(owner_ref[region] == pair, totals[region], 0.0)
    again = jnp.broadcast_to(result[:, None, :], (2, 8, 128)).reshape(16, 128)
    narrow = (iota2((128, 16), 0) % 16 == iota2((128, 16), 1)).astype(F32)
    out_ref[0] = jnp.dot(
        jnp.where(keep, again, 0.0), narrow, preferred_element_type=F32, precision=lax.Precision.HIGHEST
    )


def on_device(three_center, green, screened, block_tile, sigma_owner):
    dma = pltpu.SemaphoreType.DMA
    return pl.pallas_call(
        kernel,
        out_shape=jax.ShapeDtypeStruct((1, 16, 16), F32),
        in_specs=[pl.BlockSpec(memory_space=pltpu.HBM)] * 5,
        out_specs=pl.BlockSpec(memory_space=pltpu.VMEM),
        scratch_shapes=[
            pltpu.SMEM((6, 16), jnp.int32),
            pltpu.SMEM((16,), jnp.int32),
            pltpu.VMEM((128, 16, 384), BF16),
            pltpu.VMEM((16, 64, 64), BF16),
            pltpu.VMEM((16, 128, 384), BF16),
            pltpu.VMEM((384, 384), BF16),
            pltpu.VMEM((16, 384, 128), BF16),
            pltpu.VMEM((16, 128, 384), BF16),
            pltpu.VMEM((16, 384, 128), BF16),
            pltpu.VMEM((2048, 384), BF16),
            pltpu.VMEM((8, 2, 256, 1024), BF16),
            pltpu.VMEM((16, 128, 384), BF16),
            pltpu.VMEM((384, 2048), BF16),
            pltpu.VMEM((6, 16, 16, 64), BF16),
            pltpu.VMEM((16, 16, 384), BF16),
            pltpu.VMEM((16, 16, 384), BF16),
            pltpu.VMEM((6, 16, 384), BF16),
            pltpu.VMEM((6, 4, 16, 384), BF16),
            pltpu.VMEM((16, 2, 128), F32),
            pltpu.VMEM((16, 2, 128), F32),
            dma((5,)), dma, dma((4,)), dma, dma, dma, dma,
            dma((2, 4, 4)), dma((2, 4, 4)), dma((2, 4, 4)), dma((2, 4, 4)), dma((4,)), dma((4,)),
            dma, dma, dma((4,)), dma((4,)), dma((2,)), dma((2,)),
        ],
        compiler_params=pltpu.CompilerParams(
            collective_id=0, has_side_effects=True, vmem_limit_bytes=60 * 1024 * 1024
        ),
    )(block_tile.T, sigma_owner, three_center, green, screened)


def solution(mesh):
    in_specs = (P("pair", "ri", None, None), P("pair", None, None, None), P("ri", None), P(), P())
    return jax.shard_map(
        on_device, mesh=mesh, in_specs=in_specs, out_specs=P("pair", None, None), check_vma=False
    )
```

```python
import functools

import jax
import jax.numpy as jnp
from jax import lax
from jax.experimental import pallas as pl
from jax.experimental.pallas import tpu as pltpu
from jax.sharding import PartitionSpec as P

MESH = pl.DeviceIdType.MESH
F32, BF16 = jnp.float32, jnp.bfloat16


def remote(src, dst, send_sem, recv_sem, device):
    return pltpu.make_async_remote_copy(
        src_ref=src, dst_ref=dst, send_sem=send_sem, recv_sem=recv_sem, device_id=device, device_id_type=MESH
    )


def wait_bytes(ref, sem):
    pltpu.make_async_copy(ref, ref, sem).wait()


def iota2(shape, dim):
    return lax.broadcasted_iota(jnp.int32, shape, dim)


NT = (((1,), (1,)), ((), ()))
ORDER = (0, 1, 3, 2)


def kernel(
    tables_hbm, three_hbm, green_hbm, screened_hbm, out_ref,
    tiles_ref, three, green, by_mu, left, stage, t_out, h_out, columns, rows, weighted, halves,
    g_wide, g_out, g_in, g_own, g_all, partials, totals,
    local_sem, a_send, a_recv, t_send, t_recv, h_send, h_recv,
    ring_send, ring_recv, sib_send, sib_recv, own_send, own_recv,
    g_send, g_recv, c_send, c_recv, f_send, f_recv,
):
    pair, ri = lax.axis_index("pair"), lax.axis_index("ri")
    z, core = pair // 2, pair % 2
    y, x = ri // 4, ri % 4
    sibling = (z * 2 + 1 - core, ri)

    def chip(step):
        return (z + step + 8) % 8

    def neighbour(step):
        return (chip(step) * 2 + core, ri)

    def plane_peer(step):
        return (ri + step) % 16

    def pair_peer(step):
        return (pair + step) % 16

    load_three = pltpu.make_async_copy(three_hbm.at[0], three, local_sem.at[0])
    load_green = pltpu.make_async_copy(green_hbm.at[0], green, local_sem.at[1])
    load_tiles = pltpu.make_async_copy(tables_hbm, tiles_ref, local_sem.at[3])
    mine = pl.ds(pl.multiple_of(ri * 16, 16), 16)
    row_piece = screened_hbm.at[
        pl.ds(pl.multiple_of(z * 16, 16), 16), pl.ds(pl.multiple_of(core * 1024, 1024), 1024)
    ]
    load_rows = pltpu.make_async_copy(row_piece, rows.at[z, core, mine], local_sem.at[2])
    load_three.start()
    load_tiles.start()
    load_green.start()
    load_rows.start()
    barrier = pltpu.get_barrier_semaphore()

    @pl.loop(1, 16)
    def _(step):
        pl.semaphore_signal(barrier, inc=1, device_id=(pair, plane_peer(step)), device_id_type=MESH)
        pl.semaphore_signal(barrier, inc=1, device_id=(pair_peer(step), ri), device_id_type=MESH)

    load_green.wait()
    load_tiles.wait()
    green_rows = pl.ds(pl.multiple_of(y * 16, 16), 16)

    @pl.loop(0, 16)
    def _(region):
        for j in range(6):
            g_wide[j, region] = green[tiles_ref[j, region], green_rows, :]

    source, target = iota2((64, 384), 0), iota2((64, 384), 1)
    picked = jnp.zeros((256, 384), F32)
    for j in range(6):
        spots = (target == source + j * 64).astype(BF16)
        picked += jnp.dot(g_wide[j].reshape(256, 64), spots, preferred_element_type=F32)
    g_out[...] = picked.astype(BF16).reshape(16, 16, 384)
    g_in[pair] = g_out[pair]

    load_rows.wait()
    pl.semaphore_wait(barrier, 30)

    def offer(q):
        for dx in range(4):
            if q or dx:
                peer = ((y + 4 - q) % 4) * 4 + (x + dx) % 4
                remote(row_piece, rows.at[z, core, mine], a_send, a_recv.at[q], (pair, peer)).start()

    offer(ORDER[0])

    @pl.loop(1, 16)
    def _(step):
        peer = pair_peer(step)
        remote(g_out.at[peer], g_in.at[pair], g_send, g_recv, (peer, ri)).start()

    for q in ORDER[1:]:
        offer(q)

    first, second = iota2((256, 256), 0), iota2((256, 256), 1)
    swap = ((first % 16) * 16 + first // 16 == second).astype(BF16)
    load_three.wait()

    for chunk in range(8):
        at = pl.ds(chunk * 16, 16)
        block = three[at].reshape(256, 384)
        by_mu[:, at] = jnp.dot(swap, block, preferred_element_type=F32).astype(BF16).reshape(16, 16, 384)

    def arrange(out):
        for two in range(8):
            pieces = by_mu[2 * two:2 * two + 2].reshape(256, 384)
            block = lax.dot_general(left[...], pieces, NT, preferred_element_type=F32)
            both = [block[:, :128].reshape(16, 24, 128), block[:, 128:].reshape(16, 24, 128)]
            out[:, two * 48:two * 48 + 48] = jnp.concatenate(both, axis=1).astype(BF16)

    unit = (iota2((384, 384), 0) == iota2((384, 384), 1)).astype(BF16)
    left[...] = unit
    arrange(stage)
    own_columns = pl.ds(pl.multiple_of(ri * 128, 128), 128)
    eye = (iota2((128, 128), 0) == iota2((128, 128), 1)).astype(BF16)

    for peer in range(16):
        t_out[peer] = lax.dot_general(eye, stage[peer], NT, preferred_element_type=F32).astype(BF16)

    def part_of(step, which, q, count=64):
        return rows.at[chip(step), which, pl.ds(pl.multiple_of(((y + q) % 4) * 64, 64), count)]

    def ring(way, step, q):
        i = (1 - way) // 2
        ref = part_of(-way * (step - 1), core, q)
        return remote(ref, ref, ring_send.at[i, step - 1, q], ring_recv.at[i, step - 1, q], neighbour(way))

    def side(way, step, q):
        i = (1 - way) // 2
        ref = part_of(-way * step, core, q)
        return remote(ref, ref, sib_send.at[i, step - 1, q], sib_recv.at[i, step - 1, q], sibling)

    def own_side(q):
        ref = part_of(0, core, q)
        return remote(ref, ref, own_send.at[q], own_recv.at[q], sibling)

    def parts_at(way, step):
        if step < 4:
            return ORDER
        return ORDER[0:2] if way == 1 else ORDER[2:4]

    def begin(q):
        wait_bytes(part_of(0, core, q, 64 if q else 48), a_recv.at[q])
        for way in (1, -1):
            ring(way, 1, q).start()
        own_side(q).start()

    def send_three(step):
        peer = plane_peer(step)
        remote(t_out.at[peer], columns.at[own_columns], t_send, t_recv, (pair, peer)).start()

    begin(ORDER[0])
    pl.loop(1, 8)(send_three)

    wait_bytes(g_in.at[pl.ds(0, 15)], g_recv)
    for k in range(6):
        g_own[k] = g_in[tiles_ref[k, pair]]

    def share(step):
        peer = ((y + step) % 4) * 4 + x
        return remote(g_own, g_all.at[:, y], c_send.at[step], c_recv.at[step], (pair, peer))

    for step in (1, 3, 2):
        share(step).start()
    g_all[:, y] = g_own[...]
    pl.loop(8, 16)(send_three)
    columns[own_columns, :] = t_out[ri]
    for q in ORDER[1:]:
        begin(q)

    def serve(step):
        for q in ORDER:
            for way in (1, -1):
                if q in parts_at(way, step):
                    wait_bytes(part_of(-way * step, core, q), ring_recv.at[(1 - way) // 2, step - 1, q])
                    if step < 4 and q in parts_at(way, step + 1):
                        ring(way, step + 1, q).start()
                    side(way, step, q).start()

    def sides_in(way, step):
        for q in parts_at(way, step):
            wait_bytes(part_of(-way * step, 1 - core, q), sib_recv.at[(1 - way) // 2, step - 1, q])

    def process(step):
        piece = chip(step)
        total = jnp.dot(rows[piece, 0], columns[0:1024], preferred_element_type=F32)
        total += jnp.dot(rows[piece, 1], columns[1024:2048], preferred_element_type=F32)
        at = pl.ds(pl.multiple_of(piece * 16, 16), 16)
        weighted[:, at] = total.astype(BF16).reshape(16, 16, 384)

    serve(1)

    for step in (1, 3, 2):
        share(step).wait_recv()
    left[...] = lax.dot_general(unit, g_all[...].reshape(384, 384), NT, preferred_element_type=F32).astype(BF16)
    arrange(h_out)
    own_lanes = pl.ds(pl.multiple_of(ri * 128, 128), 128)

    @pl.loop(1, 16)
    def _(step):
        peer = plane_peer(step)
        remote(h_out.at[peer], halves.at[:, own_lanes], h_send, h_recv, (pair, peer)).start()

    halves[:, own_lanes] = h_out[ri]

    serve(2)
    wait_bytes(columns.at[pl.ds(0, 1920)], t_recv)
    for q in ORDER:
        wait_bytes(part_of(0, 1 - core, q), own_recv.at[q])
    process(0)
    for step in (1, 2):
        for way in (1, -1):
            sides_in(way, step)
            process(-way * step)
    serve(3)
    for way in (1, -1):
        sides_in(way, 3)
        process(-3 * way)
    serve(4)
    for way in (1, -1):
        sides_in(way, 4)
    process(4)
    wait_bytes(halves.at[:, pl.ds(0, 1920)], h_recv)
    gram = jnp.dot(halves[...], weighted[...].reshape(2048, 384), preferred_element_type=F32)

    masked = jnp.where(iota2((384, 384), 0) % 24 == iota2((384, 384), 1) % 24, gram, 0.0)
    folded = jnp.sum(masked.reshape(16, 24, 384), axis=1)
    spread = (iota2((384, 128), 0) // 24 == iota2((384, 128), 1) % 16).astype(F32)
    wide = jnp.dot(folded, spread, preferred_element_type=F32, precision=lax.Precision.HIGHEST)
    keep = iota2((16, 128), 1) // 16 == iota2((16, 128), 0) % 8
    partials[ri] = jnp.sum(jnp.where(keep, wide, 0.0).reshape(2, 8, 128), axis=1)

    @pl.loop(1, 16)
    def _(step):
        remote(partials.at[ri], partials.at[ri], f_send.at[0], f_recv.at[0], (pair, plane_peer(step))).start()

    wait_bytes(partials.at[pl.ds(0, 15)], f_recv.at[0])
    totals[pair] = -jnp.sum(partials[...], axis=0)

    @pl.loop(1, 16)
    def _(step):
        remote(totals.at[pair], totals.at[pair], f_send.at[1], f_recv.at[1], (pair_peer(step), ri)).start()

    wait_bytes(rows.at[z, core, pl.ds(0, 240)], a_send)
    wait_bytes(columns.at[pl.ds(0, 1920)], t_send)
    wait_bytes(halves.at[:, pl.ds(0, 1920)], h_send)
    wait_bytes(g_in.at[pl.ds(0, 15)], g_send)
    for q in ORDER:
        own_side(q).wait_send()
    for step in (1, 2, 3, 4):
        for way in (1, -1):
            for q in parts_at(way, step):
                ring(way, step, q).wait_send()
                side(way, step, q).wait_send()

    for step in (1, 3, 2):
        share(step).wait_send()
    wait_bytes(partials.at[pl.ds(0, 15)], f_send.at[0])
    wait_bytes(totals.at[pl.ds(0, 15)], f_send.at[1])
    wait_bytes(totals.at[pl.ds(0, 15)], f_recv.at[1])
    result = jnp.zeros((2, 128), F32)
    for region in range(16):
        result += jnp.where(tiles_ref[6, region] == pair, totals[region], 0.0)
    again = jnp.broadcast_to(result[:, None, :], (2, 8, 128)).reshape(16, 128)
    narrow = (iota2((128, 16), 0) % 16 == iota2((128, 16), 1)).astype(F32)
    out_ref[0] = jnp.dot(
        jnp.where(keep, again, 0.0), narrow, preferred_element_type=F32, precision=lax.Precision.HIGHEST
    )


def on_device(three_center, green, screened, block_tile, sigma_owner):
    dma = pltpu.SemaphoreType.DMA
    tables = jnp.concatenate([block_tile.T, sigma_owner[None]], axis=0)
    return pl.pallas_call(
        kernel,
        out_shape=jax.ShapeDtypeStruct((1, 16, 16), F32),
        in_specs=[pl.BlockSpec(memory_space=pltpu.HBM)] * 4,
        out_specs=pl.BlockSpec(memory_space=pltpu.VMEM),
        scratch_shapes=[
            pltpu.SMEM((7, 16), jnp.int32),
            pltpu.VMEM((128, 16, 384), BF16),
            pltpu.VMEM((16, 64, 64), BF16),
            pltpu.VMEM((16, 128, 384), BF16),
            pltpu.VMEM((384, 384), BF16),
            pltpu.VMEM((16, 384, 128), BF16),
            pltpu.VMEM((16, 128, 384), BF16),
            pltpu.VMEM((16, 384, 128), BF16),
            pltpu.VMEM((2048, 384), BF16),
            pltpu.VMEM((8, 2, 256, 1024), BF16),
            pltpu.VMEM((16, 128, 384), BF16),
            pltpu.VMEM((384, 2048), BF16),
            pltpu.VMEM((6, 16, 16, 64), BF16),
            pltpu.VMEM((16, 16, 384), BF16),
            pltpu.VMEM((16, 16, 384), BF16),
            pltpu.VMEM((6, 16, 384), BF16),
            pltpu.VMEM((6, 4, 16, 384), BF16),
            pltpu.VMEM((16, 2, 128), F32),
            pltpu.VMEM((16, 2, 128), F32),
            dma((4,)), dma, dma((4,)), dma, dma, dma, dma,
            dma((2, 4, 4)), dma((2, 4, 4)), dma((2, 4, 4)), dma((2, 4, 4)), dma((4,)), dma((4,)),
            dma, dma, dma((4,)), dma((4,)), dma((2,)), dma((2,)),
        ],
        compiler_params=pltpu.CompilerParams(
            collective_id=0, has_side_effects=True, vmem_limit_bytes=56500000
        ),
    )(tables, three_center, green, screened)


def solution(mesh):
    in_specs = (P("pair", "ri", None, None), P("pair", None, None, None), P("ri", None), P(), P())
    return jax.shard_map(
        on_device, mesh=mesh, in_specs=in_specs, out_specs=P("pair", None, None), check_vma=False
    )
```
